256 devices in a mesh: blk: 32 (over x, z), rep: 8 (over y, core).
Axes of the slice: x: 4, y: 4, z: 8, core: 2. Of those that a mesh axis runs over, the one named last changes fastest.
Arguments:
- features: bfloat16 [65536, 256], P(('blk', 'rep')), may hold values from -6 to 6
- degree: int32 [65536], P(('blk', 'rep')), may hold values from 1 to 8
- weight: bfloat16 [256, 256], replicated, may hold values from -0.375 to 0.375
- bias: float32 [256], replicated, may hold values from -3 to 3
- tile_rows: int32 [256, 192], P(('blk', 'rep')), may hold values from 0 to 15
- tile_cols: int32 [256, 192], P(('blk', 'rep')), may hold values from 0 to 63
- tile_count: int32 [256], P(('blk', 'rep')), may hold values from 48 to 192, as said below
- tile_values: bfloat16 [256, 192, 128, 128], P(('blk', 'rep')), may hold values from -0.15625 to 0.15625
- cotangent: bfloat16 [65536, 256], P(('blk', 'rep')), may hold values from -6 to 6
Outputs:
- layer_out: bfloat16 [65536, 256], P(('blk', 'rep'))
- grad_weight: float32 [256, 256], replicated
- grad_bias: float32 [256], replicated
- grad_features: bfloat16 [65536, 256], P(('blk', 'rep'))
The draws below stay inside these ranges and needn't reach their ends.
Inputs may be any that keep to these rules, and one draw needn't show every extreme that they name: `tile_count`: at least one device has all 192 slots live; every device has at least 48.
All inputs are finite; a program needn't handle non-finite values.
Results may differ from the reference program's by a relative error of at most 0.0051.
Values may be sent and summed in bfloat16 or wider, within the bound.
No kernel may reach another device: no remote copies, remote signals or barrier semaphores. Data moves between devices by JAX's collectives and lax.ppermute only.
A program may use at most 128 MiB of HBM per device.

```python
import math
import jax
import jax.numpy as jnp
import numpy as np
from jax import lax

H = 256
TILE = 128
ROWS_DEV = 256
TCAP = 192
NODES = 65536
RB = 16
CB = 64
N_BLK = 32
N_REP = 8


def draw_tile_count(key, part):
    key = jax.random.fold_in(key, 11)
    first, second = jax.random.split(key)
    devices_all = N_BLK * N_REP
    counts = jax.random.randint(first, (devices_all,), TCAP // 4, TCAP + 1)
    fullest = jax.random.randint(second, (), 0, devices_all)
    return jnp.where(jnp.arange(devices_all) == fullest, TCAP, counts).astype(jnp.int32)


def touch_ends(entries, stream_key, smallest, top_value):
    dims = entries.shape
    index_at = [jax.random.randint(jax.random.fold_in(stream_key, axis), (), 0, dims[axis]) for axis in range(len(dims))]
    entries = entries.at[tuple(index_at)].set(smallest)
    longest = dims.index(max(dims))
    index_at[longest] = (index_at[longest] + 1) % dims[longest]
    return entries.at[tuple(index_at)].set(top_value)


def levels(rng, shape, cuts, low, largest):
    factor_of, own = 1.0, jax.random.fold_in(rng, 6)
    for position, parts in cuts:
        steps = jnp.exp(jax.random.uniform(jax.random.fold_in(own, position), (parts,), jnp.float32, low / len(cuts), largest / len(cuts)))
        factor_of = factor_of * jnp.repeat(steps, shape[position] // parts).reshape([-1 if axis == position else 1 for axis in range(len(shape))])
    return factor_of


def cumulative_ranks(number_of, slope):
    portions = [(1 << 20) // math.isqrt(standing ** slope) + 1 for standing in range(1, number_of + 1)]
    deviation = 1 + sum(portions) // (1 << 30)
    return np.cumsum(np.array([max(1, weight // deviation) for weight in portions]))


def ranked(own_key, extent, amount, slope):
    table = cumulative_ranks(amount, slope)
    ticket = jax.random.randint(jax.random.fold_in(own_key, 1), extent, 0, int(table[amount - 1]))
    standing = jnp.searchsorted(jnp.asarray(table, jnp.int32), ticket, side="right")
    return jax.random.permutation(jax.random.fold_in(own_key, 2), amount)[standing].astype(jnp.int32)


def normal_values(key, extent, deviation, reach, pieces=(), kind=jnp.bfloat16):
    level = levels(key, extent, pieces, -0.22, 0.18) if pieces else 1.0
    array = jax.random.normal(key, extent, jnp.float32) * deviation * level
    return jnp.minimum(jnp.maximum(array, -reach), reach).astype(kind)


def setup_inputs(seed: int = 0) -> dict:
    keys = jax.random.split(jax.random.key(seed), 10)
    return {
        "features": normal_values(keys[0], (NODES, H), 1.0, 6.0, ((0, 256),)),
        "degree": touch_ends(jax.random.randint(keys[1], (NODES,), 1, 9), jax.random.fold_in(keys[1], 1), 1, 8).astype(jnp.int32),
        "weight": normal_values(keys[2], (H, H), H ** -0.5, 0.375),
        "bias": normal_values(keys[3], (H,), 0.5, 3.0, (), jnp.float32),
        "tile_rows": touch_ends(jax.random.randint(keys[4], (N_BLK * N_REP, TCAP), 0, RB), jax.random.fold_in(keys[4], 1), 0, RB - 1).astype(jnp.int32),
        "tile_cols": touch_ends(ranked(keys[5], (N_BLK * N_REP, TCAP), CB, 2), jax.random.fold_in(keys[5], 3), 0, CB - 1).astype(jnp.int32),
        "tile_count": draw_tile_count(jax.random.fold_in(keys[9], 71), 0),
        "tile_values": normal_values(keys[7], (N_BLK * N_REP, TCAP, TILE, TILE), (TILE * TCAP // RB) ** -0.5, 0.15625, ((0, 256),)),
        "cotangent": normal_values(keys[8], (NODES, H), 1.0, 6.0, ((0, 256),)),
    }


def reference(features, degree, weight, bias, tile_rows, tile_cols, tile_count, tile_values, cotangent):
    inv_root = lax.rsqrt(degree.astype(jnp.float32))
    scaled = (features.astype(jnp.float32) * inv_root[:, None]).astype(jnp.bfloat16)
    scaled_blocks = scaled.reshape(N_BLK, N_REP, ROWS_DEV, H)
    slot_ids = jnp.arange(TCAP, dtype=jnp.int32)
    band_ids = jnp.arange(RB, dtype=jnp.int32)
    group_ids = jnp.arange(CB, dtype=jnp.int32)
    device_ids = jnp.arange(N_BLK * N_REP, dtype=jnp.int32)

    def forward_step(aggregate, device):
        row_owner = device // N_REP
        col_group = device % N_REP
        gathered = lax.dynamic_index_in_dim(scaled_blocks, col_group, 1, keepdims=False).reshape(CB, TILE, H)
        picked = gathered[tile_cols[device]].astype(jnp.float32)
        tile_vals = tile_values[device].astype(jnp.float32)
        products = jnp.einsum('tij,tjh->tih', tile_vals, picked, precision=lax.Precision.HIGHEST)
        active = slot_ids < tile_count[device]
        selector = ((tile_rows[device][:, None] == band_ids[None, :]) & active[:, None]).astype(jnp.float32)
        contrib = jnp.einsum('tr,tih->rih', selector, products, precision=lax.Precision.HIGHEST).reshape(RB * TILE, H)
        current = lax.dynamic_index_in_dim(aggregate, row_owner, 0, keepdims=False)
        return (lax.dynamic_update_index_in_dim(aggregate, current + contrib, row_owner, 0), None)
    aggregate, _ = lax.scan(forward_step, jnp.zeros((N_BLK, RB * TILE, H), jnp.float32), device_ids)
    aggregated = (aggregate.reshape(NODES, H) * inv_root[:, None]).astype(jnp.bfloat16)
    layer_out = (jnp.dot(aggregated, weight, preferred_element_type=jnp.float32) + bias).astype(jnp.bfloat16)
    grad_weight = jnp.dot(aggregated.T, cotangent, preferred_element_type=jnp.float32)
    grad_bias = lax.optimization_barrier(jnp.sum(cotangent.astype(jnp.float32), axis=0))
    grad_scaled = (jnp.dot(cotangent, weight.T, preferred_element_type=jnp.float32) * inv_root[:, None]).astype(jnp.bfloat16)
    grad_bands = grad_scaled.reshape(N_BLK, RB, TILE, H)

    def backward_step(grad_sum, device):
        row_owner = device // N_REP
        col_group = device % N_REP
        band_rows = lax.dynamic_index_in_dim(grad_bands, row_owner, 0, keepdims=False)
        picked = band_rows[tile_rows[device]].astype(jnp.float32)
        tile_vals = tile_values[device].astype(jnp.float32)
        products = jnp.einsum('tij,tih->tjh', tile_vals, picked, precision=lax.Precision.HIGHEST)
        active = slot_ids < tile_count[device]
        selector = ((tile_cols[device][:, None] == group_ids[None, :]) & active[:, None]).astype(jnp.float32)
        contrib = jnp.einsum('tc,tjh->cjh', selector, products, precision=lax.Precision.HIGHEST).reshape(N_BLK, ROWS_DEV, H)
        current = lax.dynamic_index_in_dim(grad_sum, col_group, 1, keepdims=False)
        return (lax.dynamic_update_index_in_dim(grad_sum, current + contrib, col_group, 1), None)
    grad_sum, _ = lax.scan(backward_step, jnp.zeros((N_BLK, N_REP, ROWS_DEV, H), jnp.float32), device_ids)
    grad_features = (grad_sum.reshape(NODES, H) * inv_root[:, None]).astype(jnp.bfloat16)
    return (layer_out, grad_weight, grad_bias, grad_features)
```

```python
import jax
import jax.numpy as jnp
from jax import lax
from jax.experimental import pallas as pl
from jax.experimental.pallas import tpu as pltpu
from jax.sharding import Mesh, PartitionSpec as P

F32 = jnp.float32
BF16 = jnp.bfloat16
NX, NZ, NY, NC = 4, 8, 4, 2
H = 256
TILE = 128
TCAP = 192
BAND = 16
GROUP = 64
CHUNK = 48
UNROLL = 8
VMEM_LIMIT = 48 * 1024 * 1024
ALL = ("x", "z", "y", "c")


def tile_steps(count_ref, place_of, product_of, acc_ref, spare):
    first = pl.program_id(0) * CHUNK
    live = jnp.clip(count_ref[0] - first, 0, CHUNK)

    def step(g, carry):
        products, places = [], []
        for u in range(UNROLL):
            t = g * UNROLL + u
            slot = first + t
            places.append(jnp.where(slot < count_ref[0], place_of(slot), spare))
            products.append(product_of(t, slot))
        for u in range(UNROLL):
            acc_ref[places[u]] += products[u]
        return carry

    lax.fori_loop(0, (live + UNROLL - 1) // UNROLL, step, 0)


def clear(acc_ref):
    def zero(i, carry):
        acc_ref[i] = jnp.zeros(acc_ref.shape[1:], F32)
        return carry

    lax.fori_loop(0, acc_ref.shape[0], zero, 0)


def forward_kernel(rows, cols, count, tiles, feats, cot_t, out, grad, acc):
    @pl.when(pl.program_id(0) == 0)
    def _():
        clear(acc)

    tile_steps(
        count,
        lambda slot: rows[slot],
        lambda t, slot: jnp.dot(tiles[t], feats[cols[slot]], preferred_element_type=F32),
        acc,
        BAND,
    )

    @pl.when(pl.program_id(0) == pl.num_programs(0) - 1)
    def _():
        grad[...] = jnp.zeros(grad.shape, F32)

        def finish(i, carry):
            block = acc[i].astype(BF16)
            out[i] = block
            grad[...] += jnp.dot(cot_t[i], block, preferred_element_type=F32)
            return carry

        lax.fori_loop(0, BAND, finish, 0)


def backward_kernel(rows, cols, count, tiles, cot_t, out, acc):
    @pl.when(pl.program_id(0) == 0)
    def _():
        clear(acc)

    tile_steps(
        count,
        lambda slot: cols[slot],
        lambda t, slot: jnp.dot(cot_t[rows[slot]], tiles[t], preferred_element_type=F32),
        acc,
        GROUP,
    )

    @pl.when(pl.program_id(0) == pl.num_programs(0) - 1)
    def _():
        def finish(i, carry):
            out[i] = acc[i].astype(BF16)
            return carry

        lax.fori_loop(0, GROUP, finish, 0)


def whole(shape):
    return pl.BlockSpec(shape, lambda s, *_: (0,) * len(shape))


def tile_block():
    return pl.BlockSpec((CHUNK, TILE, TILE), lambda s, *_: (s, 0, 0))


def forward_tiles(rows, cols, count, tiles, feats, cot_t):
    return pl.pallas_call(
        forward_kernel,
        grid_spec=pltpu.PrefetchScalarGridSpec(
            num_scalar_prefetch=3,
            grid=(TCAP // CHUNK,),
            in_specs=[tile_block(), whole((GROUP, TILE, H)), whole((BAND, H, TILE))],
            out_specs=[whole((BAND, TILE, H)), whole((H, H))],
            scratch_shapes=[pltpu.VMEM((BAND + 1, TILE, H), F32)],
        ),
        out_shape=[
            jax.ShapeDtypeStruct((BAND, TILE, H), BF16),
            jax.ShapeDtypeStruct((H, H), F32),
        ],
        compiler_params=pltpu.CompilerParams(vmem_limit_bytes=VMEM_LIMIT),
        cost_estimate=pl.CostEstimate(
            flops=TCAP * 2 * TILE * TILE * H, bytes_accessed=12 << 20, transcendentals=0
        ),
        name="forward_tiles",
    )(rows, cols, count, tiles, feats, cot_t)


def backward_tiles(rows, cols, count, tiles, cot_t):
    return pl.pallas_call(
        backward_kernel,
        grid_spec=pltpu.PrefetchScalarGridSpec(
            num_scalar_prefetch=3,
            grid=(TCAP // CHUNK,),
            in_specs=[tile_block(), whole((BAND, H, TILE))],
            out_specs=whole((GROUP, H, TILE)),
            scratch_shapes=[pltpu.VMEM((GROUP + 1, H, TILE), F32)],
        ),
        out_shape=jax.ShapeDtypeStruct((GROUP, H, TILE), BF16),
        compiler_params=pltpu.CompilerParams(vmem_limit_bytes=VMEM_LIMIT),
        cost_estimate=pl.CostEstimate(
            flops=TCAP * 2 * TILE * TILE * H, bytes_accessed=12 << 20, transcendentals=0
        ),
        name="backward_tiles",
    )(rows, cols, count, tiles, cot_t)


def shift(value, axis, size, by):
    return lax.ppermute(value, axis, [(i, (i + by) % size) for i in range(size)])


def gather4(value, axis):
    return [value, shift(value, axis, 4, -1), shift(value, axis, 4, 2), shift(value, axis, 4, 1)]


def scatter4(blocks, axis):
    return [
        shift(blocks[1], axis, 4, 1),
        shift(blocks[3], axis, 4, -1),
        shift(blocks[2], axis, 4, 2),
    ]


def swap(value):
    return lax.ppermute(value, "c", [(0, 1), (1, 0)])


def shards(
    features, degree, weight, bias, tile_rows, tile_cols, tile_count, tile_values, cotangent
):
    x, y, c = lax.axis_index("x"), lax.axis_index("y"), lax.axis_index("c")
    rows, cols, tiles = tile_rows[0], tile_cols[0], tile_values[0]
    inv_root = lax.rsqrt(degree.astype(F32))
    scaled = (features.astype(F32) * inv_root[:, None]).astype(BF16)
    cot = cotangent.astype(F32)
    cot_t = (cot * inv_root[:, None]).astype(BF16).reshape(2, TILE, H).transpose(0, 2, 1)

    row_dev = rows >> 1
    row_at = ((((row_dev & 1) ^ c) * 4 + (((row_dev >> 1) - y) & 3)) << 1) | (rows & 1)
    col_dev = cols >> 1
    col_x, col_z = (((col_dev >> 3) - x) & 3), col_dev & 7
    fwd_col = ((col_z * 4 + col_x) << 1) | (cols & 1)
    bwd_col = ((col_x * 8 + col_z) << 1) | (cols & 1)

    near = jnp.concatenate(gather4(scaled, "x"))
    feats = lax.all_gather(near, "z", axis=0, tiled=True).reshape(GROUP, TILE, H)

    cot_y = jnp.concatenate(gather4(cot_t, "y"))
    cot_band = jnp.concatenate([cot_y, swap(cot_y)])

    col_terms = backward_tiles(row_at, bwd_col, tile_count, tiles, cot_band)
    col_terms = col_terms.reshape(NX, NZ, 2, H, TILE)

    def add(a, b):
        return (a.astype(F32) + b.astype(F32)).astype(BF16)

    right1 = shift(col_terms[2, :4], "x", NX, 1)
    left1 = shift(col_terms[2, 4:], "x", NX, -1)
    right2 = shift(col_terms[1, 4:], "x", NX, 1)
    left2 = shift(col_terms[3, :4], "x", NX, -1)
    right3 = shift(add(col_terms[1, :4], right1), "x", NX, 1)
    left3 = shift(add(col_terms[3, 4:], left1), "x", NX, -1)

    band_terms, grad_t = forward_tiles(row_at, fwd_col, tile_count, tiles, feats, cot_band)
    band_terms = band_terms.reshape(NC, NY, 2 * TILE, H)
    half = band_terms[0].astype(F32) + swap(band_terms[1]).astype(F32)
    half16 = half.astype(BF16)
    total = half[0]
    for part in scatter4(half16, "y"):
        total = total + part.astype(F32)
    aggregated = (total * inv_root[:, None]).astype(BF16)
    layer_out = (jnp.dot(aggregated, weight, preferred_element_type=F32) + bias).astype(BF16)

    cot_sum = jnp.sum(cot, axis=0)
    extra = jnp.zeros((8, 8, H), F32).at[:, 0].set(
        jnp.where(jnp.arange(8)[:, None] == 0, cot_sum[None, :], 0.0)
    )
    chunks = jnp.concatenate([grad_t.reshape(8, 32, H), extra], axis=1).reshape(NY, NC, 40, H)
    keep = lax.dynamic_index_in_dim(chunks, c, 1, keepdims=False)
    give = lax.dynamic_index_in_dim(chunks, 1 - c, 1, keepdims=False)
    keep = keep + swap(give)
    keep = [lax.dynamic_index_in_dim(keep, (y + o) & 3, 0, keepdims=False) for o in range(4)]
    part = keep[0]
    for other in scatter4(keep, "y"):
        part = part + other
    near_parts = gather4(part, "x")
    part = (near_parts[0] + near_parts[2]) + (near_parts[1] + near_parts[3])
    part = jnp.sum(
        lax.all_to_all(jnp.broadcast_to(part, (NZ, 40, H)), "z", 0, 0, tiled=True), axis=0
    )
    by_y = jnp.stack(gather4(part, "y"))
    by_y = jnp.take(by_y, (jnp.arange(4) - y) & 3, axis=0)
    by_c = lax.all_gather(by_y, "c", axis=1)
    grad_weight = by_c[:, :, :32].reshape(H, H).T
    grad_bias = by_c[0, 0, 32]

    own_x = jnp.concatenate(
        [
            col_terms[0, :4].astype(F32) + right3.astype(F32) + left2.astype(F32),
            col_terms[0, 4:].astype(F32) + right2.astype(F32) + left3.astype(F32),
        ]
    ).astype(BF16)
    parts = lax.all_to_all(own_x, "z", 0, 0, tiled=True)
    own = jnp.sum(parts.astype(F32), axis=0)
    grad_features = jnp.einsum(
        "ahn,gh->ang", own, weight.astype(F32), precision=lax.Precision.HIGHEST
    ).reshape(2 * TILE, H)
    grad_features = (grad_features * inv_root[:, None]).astype(BF16)
    return (layer_out, grad_weight, grad_bias, grad_features)


def solution(mesh):
    split = Mesh(mesh.devices.reshape(NX, NZ, NY, NC), ALL)
    return jax.shard_map(
        shards,
        mesh=split,
        in_specs=(
            P(ALL, None),
            P(ALL),
            P(),
            P(),
            P(ALL, None),
            P(ALL, None),
            P(ALL),
            P(ALL, None, None, None),
            P(ALL, None),
        ),
        out_specs=(P(ALL, None), P(), P(), P(ALL, None)),
        check_vma=False,
    )
```

```python
import jax
import jax.numpy as jnp
from jax import lax
from jax.experimental import pallas as pl
from jax.experimental.pallas import tpu as pltpu
from jax.sharding import Mesh, PartitionSpec as P

F32 = jnp.float32
BF16 = jnp.bfloat16
NX, NZ, NY, NC = 4, 8, 4, 2
H = 256
TILE = 128
TCAP = 192
BAND = 16
GROUP = 64
CHUNK = 48
UNROLL = 8
PART = 32
PAD = 8
VMEM_LIMIT = 48 * 1024 * 1024
ALL = ("x", "z", "y", "c")


def tile_steps(count_ref, place_of, product_of, acc_ref, spare):
    first = pl.program_id(0) * CHUNK
    live = jnp.clip(count_ref[0] - first, 0, CHUNK)

    def step(g, carry):
        products, places = [], []
        for u in range(UNROLL):
            t = g * UNROLL + u
            slot = first + t
            places.append(jnp.where(slot < count_ref[0], place_of(slot), spare))
            products.append(product_of(t, slot))
        for u in range(UNROLL):
            acc_ref[places[u]] += products[u]
        return carry

    lax.fori_loop(0, (live + UNROLL - 1) // UNROLL, step, 0)


def clear(acc_ref):
    def zero(i, carry):
        acc_ref[i] = jnp.zeros(acc_ref.shape[1:], F32)
        return carry

    lax.fori_loop(0, acc_ref.shape[0], zero, 0)


def forward_kernel(
    rows, cols, info, tiles, feats, cot_t, cot_sum, out, grad, acc, total
):
    @pl.when(pl.program_id(0) == 0)
    def _():
        clear(acc)

    tile_steps(
        info,
        lambda slot: rows[slot],
        lambda t, slot: jnp.dot(tiles[t], feats[cols[slot]], preferred_element_type=F32),
        acc,
        BAND,
    )

    @pl.when(pl.program_id(0) == pl.num_programs(0) - 1)
    def _():
        total[...] = jnp.zeros(total.shape, F32)

        def finish(i, carry):
            block = acc[i].astype(BF16)
            out[i] = block
            total[...] += jnp.dot(cot_t[i], block, preferred_element_type=F32)
            return carry

        lax.fori_loop(0, BAND, finish, 0)
        total[...] = total[...].T
        for q in range(NC * NY):
            to_c, to_y = (q // NY) ^ info[1], (q - info[2]) & 3
            grad[to_c, to_y, :PART] = total[q * PART : (q + 1) * PART]
            grad[to_c, to_y, PART:] = jnp.broadcast_to(cot_sum[...], (PAD, H))


def backward_kernel(rows, cols, count, tiles, cot_t, out, acc):
    @pl.when(pl.program_id(0) == 0)
    def _():
        clear(acc)

    tile_steps(
        count,
        lambda slot: cols[slot],
        lambda t, slot: jnp.dot(cot_t[rows[slot]], tiles[t], preferred_element_type=F32),
        acc,
        GROUP,
    )

    @pl.when(pl.program_id(0) == pl.num_programs(0) - 1)
    def _():
        def finish(i, carry):
            out[i] = acc[i].astype(BF16)
            return carry

        lax.fori_loop(0, GROUP, finish, 0)


def whole(shape):
    return pl.BlockSpec(shape, lambda s, *_: (0,) * len(shape))


def tile_block():
    return pl.BlockSpec((CHUNK, TILE, TILE), lambda s, *_: (s, 0, 0))


def forward_tiles(rows, cols, info, tiles, feats, cot_t, cot_sum):
    operands = (feats, cot_t, cot_sum)
    return pl.pallas_call(
        forward_kernel,
        grid_spec=pltpu.PrefetchScalarGridSpec(
            num_scalar_prefetch=3,
            grid=(TCAP // CHUNK,),
            in_specs=[tile_block()] + [whole(operand.shape) for operand in operands],
            out_specs=[whole((BAND, TILE, H)), whole((NC, NY, PART + PAD, H))],
            scratch_shapes=[
                pltpu.VMEM((BAND + 1, TILE, H), F32),
                pltpu.VMEM((H, H), F32),
            ],
        ),
        out_shape=[
            jax.ShapeDtypeStruct((BAND, TILE, H), BF16),
            jax.ShapeDtypeStruct((NC, NY, PART + PAD, H), F32),
        ],
        compiler_params=pltpu.CompilerParams(vmem_limit_bytes=VMEM_LIMIT),
        cost_estimate=pl.CostEstimate(
            flops=TCAP * 2 * TILE * TILE * H, bytes_accessed=12 << 20, transcendentals=0
        ),
        name="forward_tiles",
    )(rows, cols, info, tiles, *operands)


def backward_tiles(rows, cols, count, tiles, cot_t):
    return pl.pallas_call(
        backward_kernel,
        grid_spec=pltpu.PrefetchScalarGridSpec(
            num_scalar_prefetch=3,
            grid=(TCAP // CHUNK,),
            in_specs=[tile_block(), whole((BAND, H, TILE))],
            out_specs=whole((GROUP, H, TILE)),
            scratch_shapes=[pltpu.VMEM((GROUP + 1, H, TILE), F32)],
        ),
        out_shape=jax.ShapeDtypeStruct((GROUP, H, TILE), BF16),
        compiler_params=pltpu.CompilerParams(vmem_limit_bytes=VMEM_LIMIT),
        cost_estimate=pl.CostEstimate(
            flops=TCAP * 2 * TILE * TILE * H, bytes_accessed=12 << 20, transcendentals=0
        ),
        name="backward_tiles",
    )(rows, cols, count, tiles, cot_t)


def shift(value, axis, size, by):
    return lax.ppermute(value, axis, [(i, (i + by) % size) for i in range(size)])


def gather4(value, axis):
    return [value, shift(value, axis, 4, -1), shift(value, axis, 4, 2), shift(value, axis, 4, 1)]


def scatter4(blocks, axis):
    return [
        shift(blocks[1], axis, 4, 1),
        shift(blocks[3], axis, 4, -1),
        shift(blocks[2], axis, 4, 2),
    ]


def swap(value):
    return lax.ppermute(value, "c", [(0, 1), (1, 0)])


def shards(
    features, degree, weight, bias, tile_rows, tile_cols, tile_count, tile_values, cotangent
):
    x, y, c = lax.axis_index("x"), lax.axis_index("y"), lax.axis_index("c")
    rows, cols, tiles = tile_rows[0], tile_cols[0], tile_values[0]
    info = jnp.stack([tile_count[0], c, y])
    inv_root = lax.rsqrt(degree.astype(F32))
    scaled = (features.astype(F32) * inv_root[:, None]).astype(BF16).reshape(2, TILE, H)
    cot = cotangent.astype(F32)
    cot_t = (cot * inv_root[:, None]).astype(BF16).reshape(2, TILE, H).transpose(0, 2, 1)
    cot_sum = jnp.sum(cot, axis=0, keepdims=True)

    row_dev = rows >> 1
    row_at = ((((row_dev & 1) ^ c) * 4 + (((row_dev >> 1) - y) & 3)) << 1) | (rows & 1)
    col_dev = cols >> 1
    col_x, col_z = ((col_dev >> 3) - x) & 3, col_dev & 7
    fwd_col = (((col_z << 2) | col_x) << 1) | (cols & 1)
    bwd_col = (((col_x << 3) | col_z) << 1) | (cols & 1)

    near = jnp.concatenate(gather4(scaled, "x"))
    feats = lax.all_gather(near, "z", axis=0, tiled=True)

    cot_y = jnp.concatenate(gather4(cot_t, "y"))
    cot_band = jnp.concatenate([cot_y, swap(cot_y)])

    col_terms = backward_tiles(row_at, bwd_col, info, tiles, cot_band)
    col_terms = col_terms.reshape(NX, NZ, 2, H, TILE)

    def add(a, b):
        return (a.astype(F32) + b.astype(F32)).astype(BF16)

    right1 = shift(col_terms[2, :4], "x", NX, 1)
    left1 = shift(col_terms[2, 4:], "x", NX, -1)
    right2 = shift(col_terms[1, 4:], "x", NX, 1)
    left2 = shift(col_terms[3, :4], "x", NX, -1)
    right3 = shift(add(col_terms[1, :4], right1), "x", NX, 1)
    left3 = shift(add(col_terms[3, 4:], left1), "x", NX, -1)

    band_terms, part = forward_tiles(
        row_at, fwd_col, info, tiles, feats, cot_band, cot_sum
    )
    band_terms = band_terms.reshape(NC, NY, 2 * TILE, H)
    give = swap(part[1])
    band_terms, give, right2, left2, right3, left3 = lax.optimization_barrier(
        (band_terms, give, right2, left2, right3, left3)
    )

    own_x = jnp.concatenate(
        [
            col_terms[0, :4].astype(F32) + right3.astype(F32) + left2.astype(F32),
            col_terms[0, 4:].astype(F32) + right2.astype(F32) + left3.astype(F32),
        ]
    )
    own_z = lax.psum_scatter(
        own_x.reshape(NZ * 2 * H, TILE), "z", scatter_dimension=0, tiled=True
    ).reshape(2, H, TILE)

    part = part[0] + give
    own, up, across, down = [part[0]] + scatter4(part, "y")
    part = (own + across) + (up + down)
    own, up, across, down = gather4(part, "x")
    part = (own + across) + (up + down)
    half = band_terms[0].astype(F32) + swap(band_terms[1]).astype(F32)
    part, half = lax.optimization_barrier((part, half))
    part = lax.all_to_all(
        jnp.broadcast_to(part, (NZ, PART + PAD, H)), "z", 0, 0, tiled=True
    )
    part = jnp.sum(part, axis=0)
    grad_bias = part[PART]
    by_y = jnp.concatenate(gather4(part[:PART], "y"))
    by_y = lax.dynamic_slice_in_dim(jnp.concatenate([by_y, by_y]), (-y & 3) * PART, NY * PART)
    grad_weight = lax.all_gather(by_y, "c", axis=0, tiled=True)

    half16 = half.astype(BF16)
    total = half[0]
    for other in scatter4(half16, "y"):
        total = total + other.astype(F32)
    aggregated = (total * inv_root[:, None]).astype(BF16)
    layer_out = (jnp.dot(aggregated, weight, preferred_element_type=F32) + bias).astype(BF16)

    grad_features = jnp.einsum(
        "ahn,gh->ang", own_z, weight.astype(F32), precision=lax.Precision.HIGHEST
    ).reshape(2 * TILE, H)
    grad_features = (grad_features * inv_root[:, None]).astype(BF16)
    return (layer_out, grad_weight, grad_bias, grad_features)


def solution(mesh):
    split = Mesh(mesh.devices.reshape(NX, NZ, NY, NC), ALL)
    return jax.shard_map(
        shards,
        mesh=split,
        in_specs=(
            P(ALL, None),
            P(ALL),
            P(),
            P(),
            P(ALL, None),
            P(ALL, None),
            P(ALL),
            P(ALL, None, None, None),
            P(ALL, None),
        ),
        out_specs=(P(ALL, None), P(), P(), P(ALL, None)),
        check_vma=False,
    )
```

```python
import jax
import jax.numpy as jnp
from jax import lax
from jax.experimental import pallas as pl
from jax.experimental.pallas import tpu as pltpu
from jax.sharding import Mesh, PartitionSpec as P

F32 = jnp.float32
BF16 = jnp.bfloat16
NX, NZ, NY, NC = 4, 8, 4, 2
H = 256
TILE = 128
TCAP = 192
BAND = 16
GROUP = 64
CHUNK = 48
UNROLL = 16
PAD = 16
VMEM_LIMIT = 48 * 1024 * 1024
ALL = ("x", "z", "y", "c")


def tile_steps(count_ref, place_of, product_of, acc_ref, spare):
    first = pl.program_id(0) * CHUNK
    live = jnp.clip(count_ref[0] - first, 0, CHUNK)

    def step(g, carry):
        products, places = [], []
        for u in range(UNROLL):
            t = g * UNROLL + u
            slot = first + t
            places.append(jnp.where(slot < count_ref[0], place_of(slot), spare))
            products.append(product_of(t, slot))
        for u in range(UNROLL):
            acc_ref[places[u]] += products[u]
        return carry

    lax.fori_loop(0, (live + UNROLL - 1) // UNROLL, step, 0)


def clear(acc_ref):
    def zero(i, carry):
        acc_ref[i] = jnp.zeros(acc_ref.shape[1:], F32)
        return carry

    lax.fori_loop(0, acc_ref.shape[0], zero, 0)


def forward_kernel(
    rows, cols, info, tiles, feats, cot_t, cot_sum, out, grad, acc, total
):
    @pl.when(pl.program_id(0) == 0)
    def _():
        clear(acc)

    tile_steps(
        info,
        lambda slot: rows[slot],
        lambda t, slot: jnp.dot(tiles[t], feats[cols[slot]], preferred_element_type=F32),
        acc,
        BAND,
    )

    @pl.when(pl.program_id(0) == pl.num_programs(0) - 1)
    def _():
        total[...] = jnp.zeros(total.shape, F32)

        def finish(i, carry):
            block = acc[i].astype(BF16)
            out[i] = block
            total[...] += jnp.dot(cot_t[i], block, preferred_element_type=F32)
            return carry

        lax.fori_loop(0, BAND, finish, 0)
        total[...] = total[...].T
        for q in range(NC):
            to = q ^ info[1]
            grad[to, :TILE] = total[q * TILE : (q + 1) * TILE]
            grad[to, TILE:] = jnp.broadcast_to(cot_sum[...], (PAD, H))


def backward_kernel(rows, cols, count, tiles, cot_t, out, acc):
    @pl.when(pl.program_id(0) == 0)
    def _():
        clear(acc)

    tile_steps(
        count,
        lambda slot: cols[slot],
        lambda t, slot: jnp.dot(cot_t[rows[slot]], tiles[t], preferred_element_type=F32),
        acc,
        GROUP,
    )

    @pl.when(pl.program_id(0) == pl.num_programs(0) - 1)
    def _():
        def finish(i, carry):
            out[i] = acc[i].astype(BF16)
            return carry

        lax.fori_loop(0, GROUP, finish, 0)


def whole(shape):
    return pl.BlockSpec(shape, lambda s, *_: (0,) * len(shape))


def tile_block():
    return pl.BlockSpec((CHUNK, TILE, TILE), lambda s, *_: (s, 0, 0))


def forward_tiles(rows, cols, info, tiles, feats, cot_t, cot_sum):
    operands = (feats, cot_t, cot_sum)
    return pl.pallas_call(
        forward_kernel,
        grid_spec=pltpu.PrefetchScalarGridSpec(
            num_scalar_prefetch=3,
            grid=(TCAP // CHUNK,),
            in_specs=[tile_block()] + [whole(operand.shape) for operand in operands],
            out_specs=[whole((BAND, TILE, H)), whole((NC, TILE + PAD, H))],
            scratch_shapes=[
                pltpu.VMEM((BAND + 1, TILE, H), F32),
                pltpu.VMEM((H, H), F32),
            ],
        ),
        out_shape=[
            jax.ShapeDtypeStruct((BAND, TILE, H), BF16),
            jax.ShapeDtypeStruct((NC, TILE + PAD, H), F32),
        ],
        compiler_params=pltpu.CompilerParams(vmem_limit_bytes=VMEM_LIMIT),
        cost_estimate=pl.CostEstimate(
            flops=TCAP * 2 * TILE * TILE * H, bytes_accessed=12 << 20, transcendentals=0
        ),
        name="forward_tiles",
    )(rows, cols, info, tiles, *operands)


def backward_tiles(rows, cols, count, tiles, cot_t):
    return pl.pallas_call(
        backward_kernel,
        grid_spec=pltpu.PrefetchScalarGridSpec(
            num_scalar_prefetch=3,
            grid=(TCAP // CHUNK,),
            in_specs=[tile_block(), whole((BAND, H, TILE))],
            out_specs=whole((GROUP, H, TILE)),
            scratch_shapes=[pltpu.VMEM((GROUP + 1, H, TILE), F32)],
        ),
        out_shape=jax.ShapeDtypeStruct((GROUP, H, TILE), BF16),
        compiler_params=pltpu.CompilerParams(vmem_limit_bytes=VMEM_LIMIT),
        cost_estimate=pl.CostEstimate(
            flops=TCAP * 2 * TILE * TILE * H, bytes_accessed=12 << 20, transcendentals=0
        ),
        name="backward_tiles",
    )(rows, cols, count, tiles, cot_t)


def shift(value, axis, size, by):
    return lax.ppermute(value, axis, [(i, (i + by) % size) for i in range(size)])


def gather4(value, axis):
    return [value, shift(value, axis, 4, -1), shift(value, axis, 4, 2), shift(value, axis, 4, 1)]


def scatter4(blocks, axis):
    return [
        shift(blocks[1], axis, 4, 1),
        shift(blocks[3], axis, 4, -1),
        shift(blocks[2], axis, 4, 2),
    ]


def swap(value):
    return lax.ppermute(value, "c", [(0, 1), (1, 0)])


def shards(
    features, degree, weight, bias, tile_rows, tile_cols, tile_count, tile_values, cotangent
):
    x, y, c = lax.axis_index("x"), lax.axis_index("y"), lax.axis_index("c")
    rows, cols, tiles = tile_rows[0], tile_cols[0], tile_values[0]
    info = jnp.stack([tile_count[0], c])
    inv_root = lax.rsqrt(degree.astype(F32))
    scaled = (features.astype(F32) * inv_root[:, None]).astype(BF16).reshape(2, TILE, H)
    cot = cotangent.astype(F32)
    cot_t = (cot * inv_root[:, None]).astype(BF16).reshape(2, TILE, H).transpose(0, 2, 1)
    cot_sum = jnp.sum(cot, axis=0, keepdims=True)

    row_dev = rows >> 1
    row_at = ((((row_dev & 1) ^ c) * 4 + (((row_dev >> 1) - y) & 3)) << 1) | (rows & 1)
    col_dev = cols >> 1
    col_x, col_z = ((col_dev >> 3) - x) & 3, col_dev & 7
    fwd_col = (((col_z << 2) | col_x) << 1) | (cols & 1)
    bwd_col = (((col_x << 3) | col_z) << 1) | (cols & 1)

    near = jnp.concatenate(gather4(scaled, "x"))
    cot_y = jnp.concatenate(gather4(cot_t, "y"))
    near, cot_y = lax.optimization_barrier((near, cot_y))
    feats = lax.all_gather(near, "z", axis=0, tiled=True)

    cot_band = jnp.concatenate([cot_y, swap(cot_y)])

    col_terms = backward_tiles(row_at, bwd_col, info, tiles, cot_band)
    col_terms = col_terms.reshape(NX, NZ, 2, H, TILE)

    def add(a, b):
        return (a.astype(F32) + b.astype(F32)).astype(BF16)

    right1 = shift(col_terms[2, :4], "x", NX, 1)
    left1 = shift(col_terms[2, 4:], "x", NX, -1)
    right2 = shift(col_terms[1, 4:], "x", NX, 1)
    left2 = shift(col_terms[3, :4], "x", NX, -1)
    right3 = shift(add(col_terms[1, :4], right1), "x", NX, 1)
    left3 = shift(add(col_terms[3, 4:], left1), "x", NX, -1)

    own_x = jnp.concatenate(
        [
            col_terms[0, :4].astype(F32) + right3.astype(F32) + left2.astype(F32),
            col_terms[0, 4:].astype(F32) + right2.astype(F32) + left3.astype(F32),
        ]
    )
    feats, own_x = lax.optimization_barrier((feats, own_x))
    own_z = lax.psum_scatter(
        own_x.reshape(NZ * 2 * H, TILE), "z", scatter_dimension=0, tiled=True
    ).reshape(2, H, TILE)

    band_terms, part = forward_tiles(
        row_at, fwd_col, info, tiles, feats, cot_band, cot_sum
    )
    band_terms = band_terms.reshape(NC, NY, 2 * TILE, H)
    give = swap(part[1])

    part = (part[0] + give).astype(BF16)
    for axis in ("y", "x"):
        own, up, across, down = (value.astype(F32) for value in gather4(part, axis))
        part = ((own + across) + (up + down)).astype(BF16)
    half = band_terms[0].astype(F32) + swap(band_terms[1]).astype(F32)
    part, half = lax.optimization_barrier((part, half))
    own, up, down, across = (
        value.astype(F32) for value in [part] + [shift(part, "z", NZ, by) for by in (2, -2, 4)]
    )
    part = (own + across) + (up + down)
    part = part + lax.ppermute(part, "z", [(i, i ^ 1) for i in range(NZ)])
    grad_bias = part[TILE]
    grad_weight = lax.all_gather(part[:TILE], "c", axis=0, tiled=True)

    half16 = half.astype(BF16)
    total = half[0]
    for other in scatter4(half16, "y"):
        total = total + other.astype(F32)
    aggregated = (total * inv_root[:, None]).astype(BF16)
    layer_out = (jnp.dot(aggregated, weight, preferred_element_type=F32) + bias).astype(BF16)

    grad_features = jnp.einsum(
        "ahn,gh->ang", own_z, weight.astype(F32), precision=lax.Precision.HIGHEST
    ).reshape(2 * TILE, H)
    grad_features = (grad_features * inv_root[:, None]).astype(BF16)
    return (layer_out, grad_weight, grad_bias, grad_features)


def solution(mesh):
    split = Mesh(mesh.devices.reshape(NX, NZ, NY, NC), ALL)
    return jax.shard_map(
        shards,
        mesh=split,
        in_specs=(
            P(ALL, None),
            P(ALL),
            P(),
            P(),
            P(ALL, None),
            P(ALL, None),
            P(ALL),
            P(ALL, None, None, None),
            P(ALL, None),
        ),
        out_specs=(P(ALL, None), P(), P(), P(ALL, None)),
        check_vma=False,
    )
```

```python
import jax
import jax.numpy as jnp
from jax import lax
from jax.experimental import pallas as pl
from jax.experimental.pallas import tpu as pltpu
from jax.sharding import Mesh, PartitionSpec as P

F32 = jnp.float32
BF16 = jnp.bfloat16
NX, NZ, NY, NC = 4, 8, 4, 2
H = 256
TILE = 128
TCAP = 192
BAND = 16
GROUP = 64
CHUNK = 48
UNROLL = 16
PAD = 16
VMEM_LIMIT = 48 * 1024 * 1024
ALL = ("x", "z", "y", "c")


def tile_steps(count_ref, place_of, product_of, acc_ref, spare):
    first = pl.program_id(0) * CHUNK
    live = jnp.clip(count_ref[0] - first, 0, CHUNK)

    def step(g, carry):
        products, places = [], []
        for u in range(UNROLL):
            t = g * UNROLL + u
            slot = first + t
            places.append(jnp.where(slot < count_ref[0], place_of(slot), spare))
            products.append(product_of(t, slot))
        for u in range(UNROLL):
            acc_ref[places[u]] += products[u]
        return carry

    lax.fori_loop(0, (live + UNROLL - 1) // UNROLL, step, 0)


def clear(acc_ref):
    def zero(i, carry):
        acc_ref[i] = jnp.zeros(acc_ref.shape[1:], F32)
        return carry

    lax.fori_loop(0, acc_ref.shape[0], zero, 0)


def forward_kernel(
    rows, cols, info, tiles, feats, cot_t, cot_sum, out, grad, acc, total
):
    @pl.when(pl.program_id(0) == 0)
    def _():
        clear(acc)

    tile_steps(
        info,
        lambda slot: rows[slot],
        lambda t, slot: jnp.dot(tiles[t], feats[cols[slot]], preferred_element_type=F32),
        acc,
        BAND,
    )

    @pl.when(pl.program_id(0) == pl.num_programs(0) - 1)
    def _():
        total[...] = jnp.zeros(total.shape, F32)

        def finish(i, carry):
            block = acc[i].astype(BF16)
            out[i] = block
            total[...] += jnp.dot(cot_t[i], block, preferred_element_type=F32)
            return carry

        lax.fori_loop(0, BAND, finish, 0)
        total[...] = total[...].T
        for q in range(NC):
            to = q ^ info[1]
            grad[to, :TILE] = total[q * TILE : (q + 1) * TILE]
            grad[to, TILE:] = jnp.broadcast_to(cot_sum[...], (PAD, H))


def backward_kernel(rows, cols, count, tiles, cot_t, right, left, rest, acc):
    @pl.when(pl.program_id(0) == 0)
    def _():
        clear(acc)

    tile_steps(
        count,
        lambda slot: cols[slot],
        lambda t, slot: jnp.dot(cot_t[rows[slot]], tiles[t], preferred_element_type=F32),
        acc,
        GROUP,
    )

    @pl.when(pl.program_id(0) == pl.num_programs(0) - 1)
    def _():
        def finish(i, carry):
            right[i] = acc[i].astype(BF16)
            left[i] = acc[16 + i].astype(BF16)
            rest[i] = acc[32 + i].astype(BF16)
            rest[16 + i] = acc[48 + i].astype(BF16)
            return carry

        lax.fori_loop(0, 16, finish, 0)


def whole(shape):
    return pl.BlockSpec(shape, lambda s, *_: (0,) * len(shape))


def tile_block():
    return pl.BlockSpec((CHUNK, TILE, TILE), lambda s, *_: (s, 0, 0))


def forward_tiles(rows, cols, info, tiles, feats, cot_t, cot_sum):
    operands = (feats, cot_t, cot_sum)
    return pl.pallas_call(
        forward_kernel,
        grid_spec=pltpu.PrefetchScalarGridSpec(
            num_scalar_prefetch=3,
            grid=(TCAP // CHUNK,),
            in_specs=[tile_block()] + [whole(operand.shape) for operand in operands],
            out_specs=[whole((BAND, TILE, H)), whole((NC, TILE + PAD, H))],
            scratch_shapes=[
                pltpu.VMEM((BAND + 1, TILE, H), F32),
                pltpu.VMEM((H, H), F32),
            ],
        ),
        out_shape=[
            jax.ShapeDtypeStruct((BAND, TILE, H), BF16),
            jax.ShapeDtypeStruct((NC, TILE + PAD, H), F32),
        ],
        compiler_params=pltpu.CompilerParams(vmem_limit_bytes=VMEM_LIMIT),
        cost_estimate=pl.CostEstimate(
            flops=TCAP * 2 * TILE * TILE * H, bytes_accessed=12 << 20, transcendentals=0
        ),
        name="forward_tiles",
    )(rows, cols, info, tiles, *operands)


def backward_tiles(rows, cols, count, tiles, cot_t):
    return pl.pallas_call(
        backward_kernel,
        grid_spec=pltpu.PrefetchScalarGridSpec(
            num_scalar_prefetch=3,
            grid=(TCAP // CHUNK,),
            in_specs=[tile_block(), whole((BAND, H, TILE))],
            out_specs=[whole((blocks, H, TILE)) for blocks in (16, 16, 32)],
            scratch_shapes=[pltpu.VMEM((GROUP + 1, H, TILE), F32)],
        ),
        out_shape=[jax.ShapeDtypeStruct((blocks, H, TILE), BF16) for blocks in (16, 16, 32)],
        compiler_params=pltpu.CompilerParams(vmem_limit_bytes=VMEM_LIMIT),
        cost_estimate=pl.CostEstimate(
            flops=TCAP * 2 * TILE * TILE * H, bytes_accessed=12 << 20, transcendentals=0
        ),
        name="backward_tiles",
    )(rows, cols, count, tiles, cot_t)


def shift(value, axis, size, by):
    return lax.ppermute(value, axis, [(i, (i + by) % size) for i in range(size)])


def gather4(value, axis):
    return [value, shift(value, axis, 4, -1), shift(value, axis, 4, 2), shift(value, axis, 4, 1)]


def scatter4(blocks, axis):
    return [
        shift(blocks[1], axis, 4, 1),
        shift(blocks[3], axis, 4, -1),
        shift(blocks[2], axis, 4, 2),
    ]


def swap(value):
    return lax.ppermute(value, "c", [(0, 1), (1, 0)])


def shards(
    features, degree, weight, bias, tile_rows, tile_cols, tile_count, tile_values, cotangent
):
    x, y, c = lax.axis_index("x"), lax.axis_index("y"), lax.axis_index("c")
    rows, cols, tiles = tile_rows[0], tile_cols[0], tile_values[0]
    info = jnp.stack([tile_count[0], c])
    inv_root = lax.rsqrt(degree.astype(F32))
    scaled = (features.astype(F32) * inv_root[:, None]).astype(BF16).reshape(2, TILE, H)
    cot = cotangent.astype(F32)
    cot_t = (cot * inv_root[:, None]).astype(BF16).reshape(2, TILE, H).transpose(0, 2, 1)
    cot_sum = jnp.sum(cot, axis=0, keepdims=True)

    row_dev = rows >> 1
    row_at = ((((row_dev & 1) ^ c) * 4 + (((row_dev >> 1) - y) & 3)) << 1) | (rows & 1)
    col_dev = cols >> 1
    col_x, col_z = ((col_dev >> 3) - x) & 3, col_dev & 7
    fwd_col = (((col_z << 2) | col_x) << 1) | (cols & 1)
    places = {(2, 0): 0, (1, 1): 8, (2, 1): 16, (3, 0): 24, (1, 0): 32, (3, 1): 40, (0, 0): 48, (0, 1): 56}
    bwd_col = ((col_z & 3) << 1) | (cols & 1)
    for (of_x, of_z), place in places.items():
        bwd_col += jnp.where((col_x == of_x) & (col_z >> 2 == of_z), place, 0)

    near = jnp.concatenate(gather4(scaled, "x"))
    cot_y = jnp.concatenate(gather4(cot_t, "y"))
    near, cot_y = lax.optimization_barrier((near, cot_y))
    feats = lax.all_gather(near, "z", axis=0, tiled=True)

    cot_band = jnp.concatenate([cot_y, swap(cot_y)])

    to_right, to_left, kept = backward_tiles(row_at, bwd_col, info, tiles, cot_band)

    def add(a, b):
        return (a.astype(F32) + b.astype(F32)).astype(BF16)

    right1 = shift(to_right, "x", NX, 1)
    left1 = shift(to_left, "x", NX, -1)
    to_right, to_left = lax.optimization_barrier(
        (add(kept[:8], right1[:8]), add(kept[8:16], left1[:8]))
    )
    right2 = shift(to_right, "x", NX, 1)
    left2 = shift(to_left, "x", NX, -1)

    own_x = jnp.concatenate(
        [
            kept[16:24].astype(F32) + right2.astype(F32) + left1[8:].astype(F32),
            kept[24:].astype(F32) + right1[8:].astype(F32) + left2.astype(F32),
        ]
    )
    feats, own_x = lax.optimization_barrier((feats, own_x))
    own_z = lax.psum_scatter(
        own_x.reshape(NZ * 2 * H, TILE), "z", scatter_dimension=0, tiled=True
    ).reshape(2, H, TILE)

    band_terms, part = forward_tiles(
        row_at, fwd_col, info, tiles, feats, cot_band, cot_sum
    )
    band_terms = band_terms.reshape(NC, NY, 2 * TILE, H)
    give = swap(part[1])

    part = (part[0] + give).astype(BF16)
    for axis in ("y", "x"):
        own, up, across, down = (value.astype(F32) for value in gather4(part, axis))
        part = ((own + across) + (up + down)).astype(BF16)
    half = band_terms[0].astype(F32) + swap(band_terms[1]).astype(F32)
    part, half = lax.optimization_barrier((part, half))
    own, up, down, across = (
        value.astype(F32) for value in [part] + [shift(part, "z", NZ, by) for by in (2, -2, 4)]
    )
    part = (own + across) + (up + down)
    other = lax.ppermute(part, "z", [(i, i ^ 1) for i in range(NZ)])
    grad_bias = part[TILE] + other[TILE]
    part = part[:TILE] + other[:TILE]

    half16 = half.astype(BF16)
    total = half[0]
    for other in scatter4(half16, "y"):
        total = total + other.astype(F32)
    aggregated = (total * inv_root[:, None]).astype(BF16)
    layer_out = (jnp.dot(aggregated, weight, preferred_element_type=F32) + bias).astype(BF16)

    grad_features = jnp.einsum(
        "ahn,gh->ang", own_z, weight.astype(F32), precision=lax.Precision.HIGHEST
    ).reshape(2 * TILE, H)
    grad_features = (grad_features * inv_root[:, None]).astype(BF16)
    part, grad_features = lax.optimization_barrier((part, grad_features))
    grad_weight = lax.all_gather(part, "c", axis=0, tiled=True)
    return (layer_out, grad_weight, grad_bias, grad_features)


def solution(mesh):
    split = Mesh(mesh.devices.reshape(NX, NZ, NY, NC), ALL)
    return jax.shard_map(
        shards,
        mesh=split,
        in_specs=(
            P(ALL, None),
            P(ALL),
            P(),
            P(),
            P(ALL, None),
            P(ALL, None),
            P(ALL),
            P(ALL, None, None, None),
            P(ALL, None),
        ),
        out_specs=(P(ALL, None), P(), P(), P(ALL, None)),
        check_vma=False,
    )
```

```python
import jax
import jax.numpy as jnp
from jax import lax
from jax.experimental import pallas as pl
from jax.experimental.pallas import tpu as pltpu
from jax.sharding import Mesh, PartitionSpec as P

F32 = jnp.float32
BF16 = jnp.bfloat16
NX, NZ, NY, NC = 4, 8, 4, 2
H = 256
TILE = 128
TCAP = 192
BAND = 16
GROUP = 64
CHUNK = 48
UNROLL = 16
PAD = 16
VMEM_LIMIT = 48 * 1024 * 1024
ALL = ("x", "z", "y", "c")


def tile_steps(count_ref, place_of, product_of, acc_ref, spare):
    first = pl.program_id(0) * CHUNK
    live = jnp.clip(count_ref[0] - first, 0, CHUNK)

    def step(g, carry):
        products, places = [], []
        for u in range(UNROLL):
            t = g * UNROLL + u
            slot = first + t
            places.append(jnp.where(slot < count_ref[0], place_of(slot), spare))
            products.append(product_of(t, slot))
        for u in range(UNROLL):
            acc_ref[places[u]] += products[u]
        return carry

    lax.fori_loop(0, (live + UNROLL - 1) // UNROLL, step, 0)


def clear(acc_ref):
    def zero(i, carry):
        acc_ref[i] = jnp.zeros(acc_ref.shape[1:], F32)
        return carry

    lax.fori_loop(0, acc_ref.shape[0], zero, 0)


def forward_kernel(
    rows, cols, info, tiles, feats, cot_t, cot_sum, out, grad, acc, total
):
    @pl.when(pl.program_id(0) == 0)
    def _():
        clear(acc)

    tile_steps(
        info,
        lambda slot: rows[slot],
        lambda t, slot: jnp.dot(tiles[t], feats[cols[slot]], preferred_element_type=F32),
        acc,
        BAND,
    )

    @pl.when(pl.program_id(0) == pl.num_programs(0) - 1)
    def _():
        for first in (0, BAND // 2):
            products = []
            for i in range(first, first + BAND // 2, 2):
                out[i] = acc[i].astype(BF16)
                out[i + 1] = acc[i + 1].astype(BF16)
                left = jnp.concatenate([cot_t[i], cot_t[i + 1]], axis=1)
                right = jnp.concatenate([out[i], out[i + 1]], axis=0)
                products.append(jnp.dot(left, right, preferred_element_type=F32))
            product = (products[0] + products[1]) + (products[2] + products[3])
            total[...] = product if first == 0 else total[...] + product
        total[...] = total[...].T
        for q in range(NC):
            to = q ^ info[1]
            grad[to, :TILE] = total[q * TILE : (q + 1) * TILE]
            grad[to, TILE:] = jnp.broadcast_to(cot_sum[...], (PAD, H))


def backward_kernel(rows, cols, count, tiles, cot_t, right, left, rest, acc):
    @pl.when(pl.program_id(0) == 0)
    def _():
        clear(acc)

    tile_steps(
        count,
        lambda slot: cols[slot],
        lambda t, slot: jnp.dot(cot_t[rows[slot]], tiles[t], preferred_element_type=F32),
        acc,
        GROUP,
    )

    @pl.when(pl.program_id(0) == pl.num_programs(0) - 1)
    def _():
        def finish(i, carry):
            right[i] = acc[i].astype(BF16)
            left[i] = acc[16 + i].astype(BF16)
            rest[i] = acc[32 + i].astype(BF16)
            rest[16 + i] = acc[48 + i].astype(BF16)
            return carry

        lax.fori_loop(0, 16, finish, 0)


def whole(shape):
    return pl.BlockSpec(shape, lambda s, *_: (0,) * len(shape))


def tile_block():
    return pl.BlockSpec((CHUNK, TILE, TILE), lambda s, *_: (s, 0, 0))


def forward_tiles(rows, cols, info, tiles, feats, cot_t, cot_sum):
    operands = (feats, cot_t, cot_sum)
    return pl.pallas_call(
        forward_kernel,
        grid_spec=pltpu.PrefetchScalarGridSpec(
            num_scalar_prefetch=3,
            grid=(TCAP // CHUNK,),
            in_specs=[tile_block()] + [whole(operand.shape) for operand in operands],
            out_specs=[whole((BAND, TILE, H)), whole((NC, TILE + PAD, H))],
            scratch_shapes=[
                pltpu.VMEM((BAND + 1, TILE, H), F32),
                pltpu.VMEM((H, H), F32),
            ],
        ),
        out_shape=[
            jax.ShapeDtypeStruct((BAND, TILE, H), BF16),
            jax.ShapeDtypeStruct((NC, TILE + PAD, H), F32),
        ],
        compiler_params=pltpu.CompilerParams(vmem_limit_bytes=VMEM_LIMIT),
        cost_estimate=pl.CostEstimate(
            flops=TCAP * 2 * TILE * TILE * H, bytes_accessed=12 << 20, transcendentals=0
        ),
        name="forward_tiles",
    )(rows, cols, info, tiles, *operands)


def backward_tiles(rows, cols, count, tiles, cot_t):
    return pl.pallas_call(
        backward_kernel,
        grid_spec=pltpu.PrefetchScalarGridSpec(
            num_scalar_prefetch=3,
            grid=(TCAP // CHUNK,),
            in_specs=[tile_block(), whole((BAND, H, TILE))],
            out_specs=[whole((blocks, H, TILE)) for blocks in (16, 16, 32)],
            scratch_shapes=[pltpu.VMEM((GROUP + 1, H, TILE), F32)],
        ),
        out_shape=[jax.ShapeDtypeStruct((blocks, H, TILE), BF16) for blocks in (16, 16, 32)],
        compiler_params=pltpu.CompilerParams(vmem_limit_bytes=VMEM_LIMIT),
        cost_estimate=pl.CostEstimate(
            flops=TCAP * 2 * TILE * TILE * H, bytes_accessed=12 << 20, transcendentals=0
        ),
        name="backward_tiles",
    )(rows, cols, count, tiles, cot_t)


def shift(value, axis, size, by):
    return lax.ppermute(value, axis, [(i, (i + by) % size) for i in range(size)])


def gather4(value, axis):
    return [value, shift(value, axis, 4, -1), shift(value, axis, 4, 2), shift(value, axis, 4, 1)]


def scatter4(blocks, axis):
    return [
        shift(blocks[1], axis, 4, 1),
        shift(blocks[3], axis, 4, -1),
        shift(blocks[2], axis, 4, 2),
    ]


def swap(value):
    return lax.ppermute(value, "c", [(0, 1), (1, 0)])


def shards(
    features, degree, weight, bias, tile_rows, tile_cols, tile_count, tile_values, cotangent
):
    x, y, c = lax.axis_index("x"), lax.axis_index("y"), lax.axis_index("c")
    rows, cols, tiles = tile_rows[0], tile_cols[0], tile_values[0]
    info = jnp.stack([tile_count[0], c])
    inv_root = lax.rsqrt(degree.astype(F32))
    scaled = (features.astype(F32) * inv_root[:, None]).astype(BF16).reshape(2, TILE, H)
    cot = cotangent.astype(F32)
    cot_t = (cot * inv_root[:, None]).astype(BF16).reshape(2, TILE, H).transpose(0, 2, 1)
    cot_sum = jnp.sum(cot, axis=0, keepdims=True)

    row_dev = rows >> 1
    row_at = ((((row_dev & 1) ^ c) * 4 + (((row_dev >> 1) - y) & 3)) << 1) | (rows & 1)
    col_dev = cols >> 1
    col_x, col_z = ((col_dev >> 3) - x) & 3, col_dev & 7
    fwd_col = (((col_z << 2) | col_x) << 1) | (cols & 1)
    places = {(2, 0): 0, (1, 1): 8, (2, 1): 16, (3, 0): 24, (1, 0): 32, (3, 1): 40, (0, 0): 48, (0, 1): 56}
    bwd_col = ((col_z & 3) << 1) | (cols & 1)
    for (of_x, of_z), place in places.items():
        bwd_col += jnp.where((col_x == of_x) & (col_z >> 2 == of_z), place, 0)

    near = jnp.concatenate(gather4(scaled, "x"))
    cot_y = jnp.concatenate(gather4(cot_t, "y"))
    near, cot_y = lax.optimization_barrier((near, cot_y))
    feats = lax.all_gather(near, "z", axis=0, tiled=True)

    cot_band = jnp.concatenate([cot_y, swap(cot_y)])

    to_right, to_left, kept = backward_tiles(row_at, bwd_col, info, tiles, cot_band)

    def add(a, b):
        return (a.astype(F32) + b.astype(F32)).astype(BF16)

    right1 = shift(to_right, "x", NX, 1)
    left1 = shift(to_left, "x", NX, -1)
    to_right, to_left = lax.optimization_barrier(
        (add(kept[:8], right1[:8]), add(kept[8:16], left1[:8]))
    )
    right2 = shift(to_right, "x", NX, 1)
    left2 = shift(to_left, "x", NX, -1)

    own_x = jnp.concatenate(
        [
            kept[16:24].astype(F32) + right2.astype(F32) + left1[8:].astype(F32),
            kept[24:].astype(F32) + right1[8:].astype(F32) + left2.astype(F32),
        ]
    )
    feats, own_x = lax.optimization_barrier((feats, own_x))
    own_z = lax.psum_scatter(
        own_x.reshape(NZ * 2 * H, TILE), "z", scatter_dimension=0, tiled=True
    ).reshape(2, H, TILE)

    band_terms, part = forward_tiles(
        row_at, fwd_col, info, tiles, feats, cot_band, cot_sum
    )
    band_terms = band_terms.reshape(NC, NY, 2 * TILE, H)
    give = swap(part[1])

    part = (part[0] + give).astype(BF16)
    for axis in ("y", "x"):
        own, up, across, down = (value.astype(F32) for value in gather4(part, axis))
        part = ((own + across) + (up + down)).astype(BF16)
    half = band_terms[0].astype(F32) + swap(band_terms[1]).astype(F32)
    own, up, down, across = (
        value.astype(F32) for value in [part] + [shift(part, "z", NZ, by) for by in (2, -2, 4)]
    )
    part, half = lax.optimization_barrier(((own + across) + (up + down), half))
    paired = lax.ppermute(part, "z", [(i, i ^ 1) for i in range(NZ)])

    half16 = half.astype(BF16)
    total = half[0]
    for other in scatter4(half16, "y"):
        total = total + other.astype(F32)
    aggregated = (total * inv_root[:, None]).astype(BF16)
    layer_out = (jnp.dot(aggregated, weight, preferred_element_type=F32) + bias).astype(BF16)

    grad_features = jnp.einsum(
        "ahn,gh->ang", own_z, weight.astype(F32), precision=lax.Precision.HIGHEST
    ).reshape(2 * TILE, H)
    grad_features = (grad_features * inv_root[:, None]).astype(BF16)
    paired, grad_features = lax.optimization_barrier((paired, grad_features))
    grad_bias = part[TILE] + paired[TILE]
    part = part[:TILE] + paired[:TILE]
    grad_weight = lax.all_gather(part, "c", axis=0, tiled=True)
    return (layer_out, grad_weight, grad_bias, grad_features)


def solution(mesh):
    split = Mesh(mesh.devices.reshape(NX, NZ, NY, NC), ALL)
    return jax.shard_map(
        shards,
        mesh=split,
        in_specs=(
            P(ALL, None),
            P(ALL),
            P(),
            P(),
            P(ALL, None),
            P(ALL, None),
            P(ALL),
            P(ALL, None, None, None),
            P(ALL, None),
        ),
        out_specs=(P(ALL, None), P(), P(), P(ALL, None)),
        check_vma=False,
    )
```

```python
import jax
import jax.numpy as jnp
from jax import lax
from jax.experimental import pallas as pl
from jax.experimental.pallas import tpu as pltpu
from jax.sharding import Mesh, PartitionSpec as P

F32 = jnp.float32
BF16 = jnp.bfloat16
NX, NZ, NY, NC = 4, 8, 4, 2
H = 256
TILE = 128
TCAP = 192
BAND = 16
GROUP = 64
CHUNK = 48
UNROLL = 16
PAD = 16
VMEM_LIMIT = 48 * 1024 * 1024
ALL = ("x", "z", "y", "c")


def tile_steps(count_ref, place_of, product_of, acc_ref, spare):
    first = pl.program_id(0) * CHUNK
    live = jnp.clip(count_ref[0] - first, 0, CHUNK)

    def step(g, carry):
        products, places = [], []
        for u in range(UNROLL):
            t = g * UNROLL + u
            slot = first + t
            places.append(jnp.where(slot < count_ref[0], place_of(slot), spare))
            products.append(product_of(t, slot))
        for u in range(UNROLL):
            acc_ref[places[u]] += products[u]
        return carry

    lax.fori_loop(0, (live + UNROLL - 1) // UNROLL, step, 0)


def clear(acc_ref):
    def zero(i, carry):
        acc_ref[i] = jnp.zeros(acc_ref.shape[1:], F32)
        return carry

    lax.fori_loop(0, acc_ref.shape[0], zero, 0)


def forward_kernel(
    rows, cols, info, tiles, feats, cot_t, cot_sum, out, grad, acc, total
):
    @pl.when(pl.program_id(0) == 0)
    def _():
        clear(acc)

    tile_steps(
        info,
        lambda slot: rows[slot],
        lambda t, slot: jnp.dot(tiles[t], feats[cols[slot]], preferred_element_type=F32),
        acc,
        BAND,
    )

    @pl.when(pl.program_id(0) == pl.num_programs(0) - 1)
    def _():
        for first in (0, BAND // 2):
            products = []
            for i in range(first, first + BAND // 2, 2):
                out[i] = acc[i].astype(BF16)
                out[i + 1] = acc[i + 1].astype(BF16)
                left = jnp.concatenate([cot_t[i], cot_t[i + 1]], axis=1)
                right = jnp.concatenate([out[i], out[i + 1]], axis=0)
                products.append(jnp.dot(left, right, preferred_element_type=F32))
            product = (products[0] + products[1]) + (products[2] + products[3])
            total[...] = product if first == 0 else total[...] + product
        total[...] = total[...].T
        for q in range(NC):
            to = q ^ info[1]
            grad[to, :TILE] = total[q * TILE : (q + 1) * TILE]
            grad[to, TILE:] = jnp.broadcast_to(cot_sum[...], (PAD, H))


def backward_kernel(rows, cols, count, tiles, cot_t, right, left, rest, acc):
    @pl.when(pl.program_id(0) == 0)
    def _():
        clear(acc)

    tile_steps(
        count,
        lambda slot: cols[slot],
        lambda t, slot: jnp.dot(cot_t[rows[slot]], tiles[t], preferred_element_type=F32),
        acc,
        GROUP,
    )

    @pl.when(pl.program_id(0) == pl.num_programs(0) - 1)
    def _():
        def finish(i, carry):
            right[i] = acc[i].astype(BF16)
            left[i] = acc[16 + i].astype(BF16)
            rest[i] = acc[32 + i].astype(BF16)
            rest[16 + i] = acc[48 + i].astype(BF16)
            return carry

        lax.fori_loop(0, 16, finish, 0)


def whole(shape):
    return pl.BlockSpec(shape, lambda s, *_: (0,) * len(shape))


def tile_block():
    return pl.BlockSpec((CHUNK, TILE, TILE), lambda s, *_: (s, 0, 0))


def forward_tiles(rows, cols, info, tiles, feats, cot_t, cot_sum):
    operands = (feats, cot_t, cot_sum)
    return pl.pallas_call(
        forward_kernel,
        grid_spec=pltpu.PrefetchScalarGridSpec(
            num_scalar_prefetch=3,
            grid=(TCAP // CHUNK,),
            in_specs=[tile_block()] + [whole(operand.shape) for operand in operands],
            out_specs=[whole((BAND, TILE, H)), whole((NC, TILE + PAD, H))],
            scratch_shapes=[
                pltpu.VMEM((BAND + 1, TILE, H), F32),
                pltpu.VMEM((H, H), F32),
            ],
        ),
        out_shape=[
            jax.ShapeDtypeStruct((BAND, TILE, H), BF16),
            jax.ShapeDtypeStruct((NC, TILE + PAD, H), F32),
        ],
        compiler_params=pltpu.CompilerParams(vmem_limit_bytes=VMEM_LIMIT),
        cost_estimate=pl.CostEstimate(
            flops=TCAP * 2 * TILE * TILE * H, bytes_accessed=12 << 20, transcendentals=0
        ),
        name="forward_tiles",
    )(rows, cols, info, tiles, *operands)


def backward_tiles(rows, cols, count, tiles, cot_t):
    return pl.pallas_call(
        backward_kernel,
        grid_spec=pltpu.PrefetchScalarGridSpec(
            num_scalar_prefetch=3,
            grid=(TCAP // CHUNK,),
            in_specs=[tile_block(), whole((BAND, H, TILE))],
            out_specs=[whole((blocks, H, TILE)) for blocks in (16, 16, 32)],
            scratch_shapes=[pltpu.VMEM((GROUP + 1, H, TILE), F32)],
        ),
        out_shape=[jax.ShapeDtypeStruct((blocks, H, TILE), BF16) for blocks in (16, 16, 32)],
        compiler_params=pltpu.CompilerParams(vmem_limit_bytes=VMEM_LIMIT),
        cost_estimate=pl.CostEstimate(
            flops=TCAP * 2 * TILE * TILE * H, bytes_accessed=12 << 20, transcendentals=0
        ),
        name="backward_tiles",
    )(rows, cols, count, tiles, cot_t)


def shift(value, axis, size, by):
    return lax.ppermute(value, axis, [(i, (i + by) % size) for i in range(size)])


def gather4(value, axis):
    return [value, shift(value, axis, 4, -1), shift(value, axis, 4, 2), shift(value, axis, 4, 1)]


def scatter4(blocks, axis):
    return [
        shift(blocks[1], axis, 4, 1),
        shift(blocks[3], axis, 4, -1),
        shift(blocks[2], axis, 4, 2),
    ]


def swap(value):
    return lax.ppermute(value, "c", [(0, 1), (1, 0)])


def shards(
    features, degree, weight, bias, tile_rows, tile_cols, tile_count, tile_values, cotangent
):
    x, y, c = lax.axis_index("x"), lax.axis_index("y"), lax.axis_index("c")
    rows, cols, tiles = tile_rows[0], tile_cols[0], tile_values[0]
    info = jnp.stack([tile_count[0], c])
    inv_root = lax.rsqrt(degree.astype(F32))
    scaled = (features.astype(F32) * inv_root[:, None]).astype(BF16).reshape(2, TILE, H)
    cot = cotangent.astype(F32)
    cot_t = (cot * inv_root[:, None]).astype(BF16).reshape(2, TILE, H).transpose(0, 2, 1)
    cot_sum = jnp.sum(cot, axis=0, keepdims=True)

    row_dev = rows >> 1
    row_at = ((((row_dev & 1) ^ c) * 4 + (((row_dev >> 1) - y) & 3)) << 1) | (rows & 1)
    col_dev = cols >> 1
    col_x, col_z = ((col_dev >> 3) - x) & 3, col_dev & 7
    fwd_col = (((col_z << 2) | col_x) << 1) | (cols & 1)
    places = {(2, 0): 0, (1, 1): 8, (2, 1): 16, (3, 0): 24, (1, 0): 32, (3, 1): 40, (0, 0): 48, (0, 1): 56}
    bwd_col = ((col_z & 3) << 1) | (cols & 1)
    for (of_x, of_z), place in places.items():
        bwd_col += jnp.where((col_x == of_x) & (col_z >> 2 == of_z), place, 0)

    near = jnp.concatenate(gather4(scaled, "x"))
    cot_y = jnp.concatenate(gather4(cot_t, "y"))
    near, cot_y = lax.optimization_barrier((near, cot_y))
    feats = lax.all_gather(near, "z", axis=0, tiled=True)

    cot_band = jnp.concatenate([cot_y, swap(cot_y)])

    to_right, to_left, kept = backward_tiles(row_at, bwd_col, info, tiles, cot_band)

    def add(a, b):
        return (a.astype(F32) + b.astype(F32)).astype(BF16)

    right1 = shift(to_right, "x", NX, 1)
    left1 = shift(to_left, "x", NX, -1)
    to_right, to_left = lax.optimization_barrier(
        (add(kept[:8], right1[:8]), add(kept[8:16], left1[:8]))
    )
    right2 = shift(to_right, "x", NX, 1)
    left2 = shift(to_left, "x", NX, -1)

    own_x = jnp.concatenate(
        [
            kept[16:24].astype(F32) + right2.astype(F32) + left1[8:].astype(F32),
            kept[24:].astype(F32) + right1[8:].astype(F32) + left2.astype(F32),
        ]
    )
    feats, own_x = lax.optimization_barrier((feats, own_x))
    own_z = lax.psum_scatter(
        own_x.reshape(NZ * 2 * H, TILE), "z", scatter_dimension=0, tiled=True
    ).reshape(2, H, TILE)

    band_terms, part = forward_tiles(
        row_at, fwd_col, info, tiles, feats, cot_band, cot_sum
    )
    band_terms = band_terms.reshape(NC, NY, 2 * TILE, H)
    give = swap(part[1])

    part = (part[0] + give).astype(BF16)
    for axis in ("y", "x"):
        own, up, across, down = (value.astype(F32) for value in gather4(part, axis))
        part = ((own + across) + (up + down)).astype(BF16)
    half = band_terms[0].astype(F32) + swap(band_terms[1]).astype(F32)
    part, half = lax.optimization_barrier((part, half))
    own, up, down, across = (
        value.astype(F32) for value in [part] + [shift(part, "z", NZ, by) for by in (2, -2, 4)]
    )
    part = (own + across) + (up + down)
    other = lax.ppermute(part, "z", [(i, i ^ 1) for i in range(NZ)])
    grad_bias = part[TILE] + other[TILE]
    part = part[:TILE] + other[:TILE]

    half16 = half.astype(BF16)
    total = half[0]
    for other in scatter4(half16, "y"):
        total = total + other.astype(F32)
    aggregated = (total * inv_root[:, None]).astype(BF16)
    layer_out = (jnp.dot(aggregated, weight, preferred_element_type=F32) + bias).astype(BF16)

    grad_features = jnp.einsum(
        "ahn,gh->ang", own_z, weight.astype(F32), precision=lax.Precision.HIGHEST
    ).reshape(2 * TILE, H)
    grad_features = (grad_features * inv_root[:, None]).astype(BF16)
    part, grad_features = lax.optimization_barrier((part, grad_features))
    grad_weight = lax.all_gather(part, "c", axis=0, tiled=True)
    return (layer_out, grad_weight, grad_bias, grad_features)


def solution(mesh):
    split = Mesh(mesh.devices.reshape(NX, NZ, NY, NC), ALL)
    return jax.shard_map(
        shards,
        mesh=split,
        in_specs=(
            P(ALL, None),
            P(ALL),
            P(),
            P(),
            P(ALL, None),
            P(ALL, None),
            P(ALL),
            P(ALL, None, None, None),
            P(ALL, None),
        ),
        out_specs=(P(ALL, None), P(), P(), P(ALL, None)),
        check_vma=False,
    )
```
